512 devices in a mesh: gx: 16 (over y, z_hi), gy: 32 (over z_lo, x, core).
Axes of the slice: x: 4, y: 8, z: 8 (z_hi: 2, z_lo: 4; z = z_hi * 4 + z_lo), core: 2. Of those that a mesh axis runs over, the one named last changes fastest.
Arguments:
- images: float32 [131072, 1152], P(('gx', 'gy')), may hold values from -0.17677669 to 0.17677669
- texts: float32 [131072, 1152], P(('gx', 'gy')), may hold values from -0.17677669 to 0.17677669
- log_temp: float32 [1], replicated, may hold values from 1.6 to 3
- bias: float32 [1], replicated, may hold values from -3 to -1
Outputs:
- row_loss: float32 [131072], P(('gx', 'gy'))
- image_grad: float32 [131072, 1152], P(('gx', 'gy'))
- text_grad: float32 [131072, 1152], P(('gx', 'gy'))
The draws below stay inside these ranges and needn't reach their ends.
All inputs are finite; a program needn't handle non-finite values.
Results may differ from the reference program's by a relative error of at most 0.00011.
Values sent between devices are 32-bit elements; how exact they have to be, the bound alone decides.
A program may use at most 64 MiB of HBM per device.

```python
import jax
import jax.numpy as jnp
from jax import lax

D = 1152
ROWS = 256
STEPS = 4
TOKENS = 131072


def block_scale(key, extent, split, low, high):
    loudness = 1.0
    for axis_at, blocks in split:
        draws = jax.random.uniform(jax.random.fold_in(jax.random.fold_in(key, 6), axis_at), (blocks,), jnp.float32, low / len(split), high / len(split))
        loudness = loudness * jnp.repeat(jnp.exp(draws), extent[axis_at] // blocks).reshape((-1,) + (1,) * (len(extent) - 1 - axis_at))
    return loudness


def gaussian(rng, shape, width, most, cuts=(), held_as=jnp.bfloat16):
    array = jax.random.normal(rng, shape, jnp.float32) * width
    if len(cuts) > 0:
        array = block_scale(rng, shape, cuts, -0.22, 0.18) * array
    return jnp.clip(array, min=-most, max=most).astype(held_as)


def setup_inputs(seed: int = 0) -> dict:
    splits = jax.random.split(jax.random.key(seed), 5)
    return {
        "images": gaussian(splits[0], (TOKENS, D), (D ** -0.5), 0.17677669, ((0, 512),), jnp.float32),
        "texts": gaussian(splits[1], (TOKENS, D), (D ** -0.5), 0.17677669, ((0, 512),), jnp.float32),
        "log_temp": jnp.clip(jax.random.uniform(splits[2], (1,), jnp.float32, 1.6, 3.0), 1.6, 3.0),
        "bias": jnp.clip(jax.random.uniform(splits[3], (1,), jnp.float32, -3.0, -1.0), -3.0, -1.0),
    }


def reference(images, texts, log_temp, bias):
    blocks = images.shape[0] // ROWS
    temp = jnp.exp(log_temp[0])
    shift_b = bias[0]
    img = images.reshape(blocks, ROWS, D)
    txt = texts.reshape(blocks, ROWS, D)
    eye = jnp.eye(ROWS, dtype=jnp.float32)
    row_sum = jnp.zeros((blocks, ROWS), jnp.float32)
    img_grad = jnp.zeros((blocks, ROWS, D), jnp.float32)
    txt_grad = jnp.zeros((blocks, ROWS, D), jnp.float32)
    for step in range(STEPS):
        partner = jnp.roll(txt, step, axis=0)
        logits = temp * jnp.einsum("prd,pcd->prc", img, partner, precision=lax.Precision.HIGHEST) + shift_b
        if step == 0:
            signs = 2.0 * eye - 1.0
            positive = eye
        else:
            signs = -jnp.ones((ROWS, ROWS), jnp.float32)
            positive = jnp.zeros((ROWS, ROWS), jnp.float32)
        row_sum = row_sum + jnp.sum(jax.nn.softplus(-signs * logits), axis=2)
        coeff = jax.nn.sigmoid(logits) - positive
        img_grad = img_grad + temp * jnp.einsum("prc,pcd->prd", coeff, partner, precision=lax.Precision.HIGHEST)
        part = temp * jnp.einsum("prc,prd->pcd", coeff, img, precision=lax.Precision.HIGHEST)
        txt_grad = txt_grad + jnp.roll(part, -step, axis=0)
    row_loss = (row_sum / (STEPS * ROWS)).reshape(-1)
    return row_loss, img_grad.reshape(-1, D), txt_grad.reshape(-1, D)
```

```python
import functools

import jax
import jax.numpy as jnp
from jax import lax
from jax.experimental import pallas as pl
from jax.experimental.pallas import tpu as pltpu
from jax.sharding import PartitionSpec as P

STEPS = 4
MESH = pl.DeviceIdType.MESH
F32 = jnp.float32
BF16 = jnp.bfloat16
CHUNKS = 2


def split(x):
    high = x.astype(BF16)
    return high, (x - high.astype(F32)).astype(BF16)


def dot3(a, b, dims):
    dot = functools.partial(
        lax.dot_general, dimension_numbers=(dims, ((), ())), preferred_element_type=F32
    )
    return dot(a[0], b[0]) + (dot(a[0], b[1]) + dot(a[1], b[0]))


def kernel(
    nx, ny, images, texts, log_temp, bias, row_loss, image_grad, text_grad,
    held, high, low, grad, loss, load_sem, send_sem, recv_sem,
):
    rows, width = images.shape
    part = rows // CHUNKS
    total = nx * ny
    me = lax.axis_index("gx") * ny + lax.axis_index("gy")
    core = lax.rem(me, 2)
    sign = 1 - 2 * core

    def at(p):
        p = lax.rem(p + total, total)
        return (p // ny, lax.rem(p, ny))

    mate, behind = at(me + sign), at(me - sign)
    ahead, back2 = at(me + 2 * sign), at(me - 2 * sign)

    loads = [
        pltpu.make_async_copy(texts, held.at[0, 0], load_sem.at[0]),
        pltpu.make_async_copy(images, held.at[1, 0], load_sem.at[1]),
    ]
    for load in loads:
        load.start()

    barrier = pltpu.get_barrier_semaphore()
    for device in (mate, behind, back2):
        pl.semaphore_signal(barrier, inc=1, device_id=device, device_id_type=MESH)
    for load in loads:
        load.wait()
    pl.semaphore_wait(barrier, 3)

    def copy(kind, stream, source, target, chunk, device):
        here = pl.ds(chunk * part, part)
        return pltpu.make_async_remote_copy(
            src_ref=held.at[stream, source, here],
            dst_ref=held.at[stream, target, here],
            send_sem=send_sem.at[kind, chunk],
            recv_sem=recv_sem.at[stream, target, chunk],
            device_id=device,
            device_id_type=MESH,
        )

    def own_to_next(chunk):
        return copy(0, 1 - core, 0, 1, chunk, behind)

    def own_to_ahead(chunk):
        return copy(1, core, 0, 2, chunk, ahead)

    def own_to_mate(chunk):
        return copy(2, core, 0, 1, chunk, mate)

    def pass_ahead(chunk):
        return copy(3, core, 1, 3, chunk, ahead)

    def relay_first(chunk):
        return copy(4, core, 1, 2, chunk, mate)

    def relay_second(chunk):
        return copy(5, core, 2, 3, chunk, mate)

    for chunk in range(CHUNKS):
        own_to_next(chunk).start()
    for chunk in range(CHUNKS):
        own_to_ahead(chunk).start()
    for chunk in range(CHUNKS):
        own_to_mate(chunk).start()

    for stream in range(2):
        high[stream], low[stream] = split(held[1 - stream, 0])
    grad[...] = jnp.zeros_like(grad)
    loss[...] = jnp.zeros_like(loss)
    temp = jnp.exp(jnp.full((1, part), log_temp[0], F32))
    shift = jnp.full((1, part), bias[0], F32)

    def unit(u, carry):
        block, chunk = u // CHUNKS, lax.rem(u, CHUNKS)
        slot = block // 2
        stream = lax.rem(core + 1 + block, 2)

        @pl.when(block >= 2)
        def _():
            here = pl.ds(chunk * part, part)
            pltpu.make_async_copy(
                held.at[stream, slot, here], held.at[stream, slot, here],
                recv_sem.at[stream, slot, chunk],
            ).wait()

        @pl.when(block == 3)
        def _():
            pass_ahead(chunk).start()
            relay_first(chunk).start()

        @pl.when(block == 5)
        def _():
            relay_second(chunk).start()

        start = pl.multiple_of(chunk * part, part)
        other = split(held[stream, slot, pl.ds(start, part), :])
        mine = (high[stream], low[stream])
        logits = temp * dot3(mine, other, ((1,), (1,))) + shift
        row = lax.broadcasted_iota(jnp.int32, (rows, part), 0)
        column = lax.broadcasted_iota(jnp.int32, (rows, part), 1)
        positive = jnp.logical_and(row == column + start, slot == 0)
        small = jnp.exp(-jnp.abs(logits))
        signed = jnp.where(positive, -logits, logits)
        loss[stream] += jnp.maximum(signed, 0.0) + jnp.log1p(small)
        sigmoid = jnp.where(logits >= 0, 1.0, small) / (1.0 + small)
        coeff = temp * jnp.where(positive, sigmoid - 1.0, sigmoid)
        grad[stream] += dot3(split(coeff), other, ((1,), (0,)))
        return carry

    lax.fori_loop(0, 2 * STEPS * CHUNKS, unit, 0)

    image_grad[...] = grad[0]
    text_grad[...] = grad[1]
    row_loss[...] = jnp.sum(loss[0].T, axis=0) / (STEPS * rows)
    for chunk in range(CHUNKS):
        for make in (own_to_next, own_to_ahead, own_to_mate, pass_ahead, relay_first, relay_second):
            make(chunk).wait_send()


def solution(mesh):
    nx, ny = mesh.shape["gx"], mesh.shape["gy"]

    def per_device(images, texts, log_temp, bias):
        rows, width = images.shape
        part = rows // CHUNKS
        vmem = pl.BlockSpec(memory_space=pltpu.VMEM)
        smem = pl.BlockSpec(memory_space=pltpu.SMEM)
        hbm = pl.BlockSpec(memory_space=pl.ANY)
        return pl.pallas_call(
            functools.partial(kernel, nx, ny),
            out_shape=(
                jax.ShapeDtypeStruct((rows,), F32),
                jax.ShapeDtypeStruct((rows, width), F32),
                jax.ShapeDtypeStruct((rows, width), F32),
            ),
            in_specs=[hbm, hbm, smem, smem],
            out_specs=(vmem, vmem, vmem),
            scratch_shapes=[
                pltpu.VMEM((2, STEPS, rows, width), F32),
                pltpu.VMEM((2, rows, width), BF16),
                pltpu.VMEM((2, rows, width), BF16),
                pltpu.VMEM((2, rows, width), F32),
                pltpu.VMEM((2, rows, part), F32),
                pltpu.SemaphoreType.DMA((2,)),
                pltpu.SemaphoreType.DMA((6, CHUNKS)),
                pltpu.SemaphoreType.DMA((2, STEPS, CHUNKS)),
            ],
            compiler_params=pltpu.CompilerParams(
                collective_id=0, has_side_effects=True, vmem_limit_bytes=48 << 20
            ),
        )(images, texts, log_temp, bias)

    return jax.shard_map(
        per_device,
        mesh=mesh,
        in_specs=(P(("gx", "gy"), None), P(("gx", "gy"), None), P(), P()),
        out_specs=(P(("gx", "gy")), P(("gx", "gy"), None), P(("gx", "gy"), None)),
        check_vma=False,
    )
```

```python
import functools

import jax
import jax.numpy as jnp
from jax import lax
from jax.experimental import pallas as pl
from jax.experimental.pallas import tpu as pltpu
from jax.sharding import PartitionSpec as P

STEPS = 4
MESH = pl.DeviceIdType.MESH
F32 = jnp.float32
BF16 = jnp.bfloat16
CHUNKS = 2
NT = ((1,), (1,))
NN = ((1,), (0,))


def split(x):
    high = x.astype(BF16)
    return high, (x - high.astype(F32)).astype(BF16)


def dot(a, b, dims):
    return lax.dot_general(a, b, (dims, ((), ())), preferred_element_type=F32)


def dot3(a, b, dims):
    return dot(a[0], b[0], dims) + (dot(a[0], b[1], dims) + dot(a[1], b[0], dims))


def kernel(
    nx, ny, images, texts, scalars, row_loss, image_grad, text_grad,
    held, high, low, grad, loss, load_sem, send_sem, recv_sem,
):
    rows, width = images.shape
    part = rows // CHUNKS
    total = nx * ny
    me = lax.axis_index("gx") * ny + lax.axis_index("gy")
    core = lax.rem(me, 2)
    sign = 1 - 2 * core

    def at(p):
        p = lax.rem(p + total, total)
        return (p // ny, lax.rem(p, ny))

    mate, behind = at(me + sign), at(me - sign)
    ahead, back2 = at(me + 2 * sign), at(me - 2 * sign)

    loads = [
        pltpu.make_async_copy(texts, held.at[0, 0], load_sem.at[0]),
        pltpu.make_async_copy(images, held.at[1, 0], load_sem.at[1]),
    ]
    for load in loads:
        load.start()

    barrier = pltpu.get_barrier_semaphore()
    for device in (mate, behind, back2):
        pl.semaphore_signal(barrier, inc=1, device_id=device, device_id_type=MESH)
    pl.semaphore_wait(barrier, 3)

    def copy(kind, stream, source, target, chunk, device):
        here = pl.ds(chunk * part, part)
        if source is None:
            source = held.at[stream, target - 1]
        return pltpu.make_async_remote_copy(
            src_ref=source.at[here],
            dst_ref=held.at[stream, target, here],
            send_sem=send_sem.at[kind, chunk],
            recv_sem=recv_sem.at[stream, target, chunk],
            device_id=device,
            device_id_type=MESH,
        )

    def own_to_next(chunk, mine, other):
        return copy(0, 1 - core, other, 1, chunk, behind)

    def own_to_ahead(chunk, mine, other):
        return copy(1, core, mine, 2, chunk, ahead)

    def own_to_mate(chunk, mine, other):
        return copy(2, core, mine, 1, chunk, mate)

    def pass_ahead(chunk):
        return copy(3, core, held.at[core, 1], 3, chunk, ahead)

    def relay_first(chunk):
        return copy(4, core, held.at[core, 1], 2, chunk, mate)

    def relay_second(chunk):
        return copy(5, core, held.at[core, 2], 3, chunk, mate)

    for which, mine, other in ((0, texts, images), (1, images, texts)):

        @pl.when(core == which)
        def _():
            for make in (own_to_next, own_to_ahead, own_to_mate):
                for chunk in range(CHUNKS):
                    make(chunk, mine, other).start()

    for load in loads:
        load.wait()
    for stream in range(2):
        high[stream], low[stream] = split(held[1 - stream, 0])
    grad[...] = jnp.zeros_like(grad)
    loss[...] = jnp.zeros_like(loss)
    temp = jnp.exp(scalars[0:1, :])
    shift = scalars[1:2, :]

    def arrived(stream, slot, chunk):
        here = held.at[stream, slot, pl.ds(chunk * part, part)]
        pltpu.make_async_copy(here, here, recv_sem.at[stream, slot, chunk]).wait()

    def coefficients(logits, positive):
        logits = temp * logits + shift
        small = jnp.exp(-jnp.abs(logits))
        sigmoid = jnp.where(logits >= 0, 1.0, small) / (1.0 + small)
        if positive is None:
            return jnp.maximum(logits, 0.0) + jnp.log1p(small), temp * sigmoid
        signed = jnp.where(positive, -logits, logits)
        losses = jnp.maximum(signed, 0.0) + jnp.log1p(small)
        return losses, temp * jnp.where(positive, sigmoid - 1.0, sigmoid)

    def whole(block, carry):
        slot = block // 2
        stream = lax.rem(core + 1 + block, 2)
        for chunk in range(CHUNKS):

            @pl.when(block >= 2)
            def _():
                arrived(stream, slot, chunk)

            @pl.when(block == 3)
            def _():
                pass_ahead(chunk).start()
                relay_first(chunk).start()

            @pl.when(block == 5)
            def _():
                relay_second(chunk).start()

        other = split(held[stream, slot])
        logits = dot3((high[stream], low[stream]), other, NT)
        pieces = []
        for chunk in range(CHUNKS):
            here = slice(chunk * part, (chunk + 1) * part)
            row = lax.broadcasted_iota(jnp.int32, (rows, part), 0)
            column = lax.broadcasted_iota(jnp.int32, (rows, part), 1) + chunk * part
            positive = jnp.logical_and(row == column, slot == 0)
            losses, coeff = coefficients(logits[:, here], positive)
            loss[stream] += losses
            pieces.append(coeff)
        grad[stream] += dot3(split(jnp.concatenate(pieces, axis=1)), other, NN)
        return carry

    def last(chunk, carry):
        arrived(core, STEPS - 1, chunk)
        start = pl.multiple_of(chunk * part, part)
        far, near = split(held[core, STEPS - 1, pl.ds(start, part), :])
        both = dot(high[core], jnp.concatenate([far, near], axis=0), NT)
        logits = both[:, :part] + both[:, part:] + dot(low[core], far, NT)
        losses, coeff = coefficients(logits, None)
        loss[core] += losses
        top, rest = split(coeff)
        grad[core] += dot(
            jnp.concatenate([top, rest], axis=1), jnp.concatenate([far, far], axis=0), NN
        ) + dot(top, near, NN)
        return carry

    lax.fori_loop(0, 2 * STEPS - 1, whole, 0)
    lax.fori_loop(0, CHUNKS, last, 0)

    image_grad[...] = grad[0]
    text_grad[...] = grad[1]
    row_loss[...] = jnp.sum(loss[0].T, axis=0) / (STEPS * rows)
    for chunk in range(CHUNKS):
        for make in (own_to_next, own_to_ahead, own_to_mate):
            make(chunk, texts, texts).wait_send()
        for make in (pass_ahead, relay_first, relay_second):
            make(chunk).wait_send()


def solution(mesh):
    nx, ny = mesh.shape["gx"], mesh.shape["gy"]

    def per_device(images, texts, log_temp, bias):
        rows, width = images.shape
        part = rows // CHUNKS
        vmem = pl.BlockSpec(memory_space=pltpu.VMEM)
        hbm = pl.BlockSpec(memory_space=pltpu.HBM)
        return pl.pallas_call(
            functools.partial(kernel, nx, ny),
            out_shape=(
                jax.ShapeDtypeStruct((rows,), F32),
                jax.ShapeDtypeStruct((rows, width), F32),
                jax.ShapeDtypeStruct((rows, width), F32),
            ),
            in_specs=[hbm, hbm, vmem],
            out_specs=(vmem, vmem, vmem),
            scratch_shapes=[
                pltpu.VMEM((2, STEPS, rows, width), F32),
                pltpu.VMEM((2, rows, width), BF16),
                pltpu.VMEM((2, rows, width), BF16),
                pltpu.VMEM((2, rows, width), F32),
                pltpu.VMEM((2, rows, part), F32),
                pltpu.SemaphoreType.DMA((2,)),
                pltpu.SemaphoreType.DMA((6, CHUNKS)),
                pltpu.SemaphoreType.DMA((2, STEPS, CHUNKS)),
            ],
            compiler_params=pltpu.CompilerParams(
                collective_id=0, has_side_effects=True, vmem_limit_bytes=51 << 20
            ),
        )(images, texts, jnp.stack([jnp.broadcast_to(log_temp, (part,)), jnp.broadcast_to(bias, (part,))]))

    return jax.shard_map(
        per_device,
        mesh=mesh,
        in_specs=(P(("gx", "gy"), None), P(("gx", "gy"), None), P(), P()),
        out_specs=(P(("gx", "gy")), P(("gx", "gy"), None), P(("gx", "gy"), None)),
        check_vma=False,
    )
```

```python
import functools

import jax
import jax.numpy as jnp
from jax import lax
from jax.experimental import pallas as pl
from jax.experimental.pallas import tpu as pltpu
from jax.sharding import PartitionSpec as P

STEPS = 4
MESH = pl.DeviceIdType.MESH
F32 = jnp.float32
BF16 = jnp.bfloat16
CHUNKS = 2
NT = ((1,), (1,))
NN = ((1,), (0,))


def split(x):
    high = x.astype(BF16)
    return high, (x - high.astype(F32)).astype(BF16)


def dot(a, b, dims):
    return lax.dot_general(a, b, (dims, ((), ())), preferred_element_type=F32)


def dot3(a, b, dims):
    return dot(a[0], b[0], dims) + (dot(a[0], b[1], dims) + dot(a[1], b[0], dims))


def kernel(
    nx, ny, images, texts, scalars, row_loss, image_grad, text_grad,
    held, high, low, grad, loss, load_sem, send_sem, recv_sem,
):
    rows, width = images.shape
    part = rows // CHUNKS
    total = nx * ny
    me = lax.axis_index("gx") * ny + lax.axis_index("gy")
    core = lax.rem(me, 2)
    sign = 1 - 2 * core

    def at(p):
        p = lax.rem(p + total, total)
        return (p // ny, lax.rem(p, ny))

    mate, behind = at(me + sign), at(me - sign)
    ahead, back2 = at(me + 2 * sign), at(me - 2 * sign)

    loads = [
        pltpu.make_async_copy(texts, held.at[0, 0], load_sem.at[0]),
        pltpu.make_async_copy(images, held.at[1, 0], load_sem.at[1]),
    ]
    for load in loads:
        load.start()

    barrier = pltpu.get_barrier_semaphore()
    for device in (mate, behind, back2):
        pl.semaphore_signal(barrier, inc=1, device_id=device, device_id_type=MESH)
    pl.semaphore_wait(barrier, 3)

    def copy(kind, stream, source, target, chunk, device):
        here = pl.ds(chunk * part, part)
        if source is None:
            source = held.at[stream, target - 1]
        return pltpu.make_async_remote_copy(
            src_ref=source.at[here],
            dst_ref=held.at[stream, target, here],
            send_sem=send_sem.at[kind, chunk],
            recv_sem=recv_sem.at[stream, target, chunk],
            device_id=device,
            device_id_type=MESH,
        )

    def own_to_next(chunk, mine, other):
        return copy(0, 1 - core, other, 1, chunk, behind)

    def own_to_ahead(chunk, mine, other):
        return copy(1, core, mine, 2, chunk, ahead)

    def own_to_mate(chunk, mine, other):
        return copy(2, core, mine, 1, chunk, mate)

    def pass_ahead(chunk):
        return copy(3, core, held.at[core, 1], 3, chunk, ahead)

    def relay_first(chunk):
        return copy(4, core, held.at[core, 1], 2, chunk, mate)

    def relay_second(chunk):
        return copy(5, core, held.at[core, 2], 3, chunk, mate)

    for which, mine, other in ((0, texts, images), (1, images, texts)):

        @pl.when(core == which)
        def _():
            for make in (own_to_next, own_to_ahead, own_to_mate):
                for chunk in range(CHUNKS):
                    make(chunk, mine, other).start()

    for load in loads:
        load.wait()
    for stream in range(2):
        high[stream], low[stream] = split(held[1 - stream, 0])
    grad[...] = jnp.zeros_like(grad)
    loss[...] = jnp.zeros_like(loss)
    temp = jnp.exp(scalars[0:1, :])
    shift = scalars[1:2, :]

    def arrived(stream, slot, chunk):
        here = held.at[stream, slot, pl.ds(chunk * part, part)]
        pltpu.make_async_copy(here, here, recv_sem.at[stream, slot, chunk]).wait()

    def coefficients(logits, positive):
        logits = temp * logits + shift
        small = jnp.exp(-jnp.abs(logits))
        sigmoid = jnp.where(logits >= 0, 1.0, small) / (1.0 + small)
        if positive is None:
            return jnp.maximum(logits, 0.0) + jnp.log1p(small), temp * sigmoid
        signed = jnp.where(positive, -logits, logits)
        losses = jnp.maximum(signed, 0.0) + jnp.log1p(small)
        return losses, temp * jnp.where(positive, sigmoid - 1.0, sigmoid)

    def whole(block, carry):
        slot = block // 2
        stream = lax.rem(core + 1 + block, 2)
        for chunk in range(CHUNKS):

            @pl.when(block >= 2)
            def _():
                arrived(stream, slot, chunk)

            @pl.when(block == 3)
            def _():
                pass_ahead(chunk).start()
                relay_first(chunk).start()

            @pl.when(block == 5)
            def _():
                relay_second(chunk).start()

        other = split(held[stream, slot])
        logits = dot3((high[stream], low[stream]), other, NT)
        pieces = []
        for chunk in range(CHUNKS):
            here = slice(chunk * part, (chunk + 1) * part)
            row = lax.broadcasted_iota(jnp.int32, (rows, part), 0)
            column = lax.broadcasted_iota(jnp.int32, (rows, part), 1) + chunk * part
            positive = jnp.logical_and(row == column, slot == 0)
            losses, coeff = coefficients(logits[:, here], positive)
            loss[stream] += losses
            pieces.append(coeff)
        grad[stream] += dot3(split(jnp.concatenate(pieces, axis=1)), other, NN)
        return carry

    def last(chunk, carry):
        arrived(core, STEPS - 1, chunk)
        start = pl.multiple_of(chunk * part, part)
        far, near = split(held[core, STEPS - 1, pl.ds(start, part), :])
        both = dot(high[core], jnp.concatenate([far, near], axis=0), NT)
        logits = both[:, :part] + both[:, part:] + dot(low[core], far, NT)
        losses, coeff = coefficients(logits, None)
        loss[core] += losses
        top, rest = split(coeff)
        grad[core] += dot(
            jnp.concatenate([top, rest], axis=1), jnp.concatenate([far, far], axis=0), NN
        ) + dot(top, near, NN)
        return carry

    lax.fori_loop(0, 2 * STEPS - 1, whole, 0)
    lax.fori_loop(0, CHUNKS, last, 0)

    image_grad[...] = grad[0]
    text_grad[...] = grad[1]
    row_loss[...] = jnp.sum(loss[0].T, axis=0) / (STEPS * rows)
    for chunk in range(CHUNKS):
        for make in (own_to_next, own_to_ahead, own_to_mate):
            make(chunk, texts, texts).wait_send()
        for make in (pass_ahead, relay_first, relay_second):
            make(chunk).wait_send()


def finish(losses, first, second, row_loss, image_grad, text_grad, sem):
    copies = [
        pltpu.make_async_copy(first, image_grad, sem.at[0]),
        pltpu.make_async_copy(second, text_grad, sem.at[1]),
        pltpu.make_async_copy(losses, row_loss, sem.at[2]),
    ]
    for copy in copies:
        copy.start()
    for copy in copies:
        copy.wait()


def solution(mesh):
    nx, ny = mesh.shape["gx"], mesh.shape["gy"]

    def per_device(images, texts, log_temp, bias):
        rows, width = images.shape
        part = rows // CHUNKS
        vmem = pl.BlockSpec(memory_space=pltpu.VMEM)
        hbm = pl.BlockSpec(memory_space=pltpu.HBM)
        shapes = (
            jax.ShapeDtypeStruct((rows,), F32),
            jax.ShapeDtypeStruct((rows, width), F32),
            jax.ShapeDtypeStruct((rows, width), F32),
        )
        results = pl.pallas_call(
            functools.partial(kernel, nx, ny),
            out_shape=shapes,
            in_specs=[hbm, hbm, vmem],
            out_specs=(vmem, vmem, vmem),
            scratch_shapes=[
                pltpu.VMEM((2, STEPS, rows, width), F32),
                pltpu.VMEM((2, rows, width), BF16),
                pltpu.VMEM((2, rows, width), BF16),
                pltpu.VMEM((2, rows, width), F32),
                pltpu.VMEM((2, rows, part), F32),
                pltpu.SemaphoreType.DMA((2,)),
                pltpu.SemaphoreType.DMA((6, CHUNKS)),
                pltpu.SemaphoreType.DMA((2, STEPS, CHUNKS)),
            ],
            compiler_params=pltpu.CompilerParams(
                collective_id=0, has_side_effects=True, vmem_limit_bytes=51 << 20
            ),
        )(images, texts, jnp.stack([jnp.broadcast_to(log_temp, (part,)), jnp.broadcast_to(bias, (part,))]))
        return pl.pallas_call(
            finish,
            out_shape=shapes,
            in_specs=[vmem] * 3,
            out_specs=(hbm, hbm, hbm),
            scratch_shapes=[pltpu.SemaphoreType.DMA((3,))],
            compiler_params=pltpu.CompilerParams(vmem_limit_bytes=8 << 20),
        )(*results)

    return jax.shard_map(
        per_device,
        mesh=mesh,
        in_specs=(P(("gx", "gy"), None), P(("gx", "gy"), None), P(), P()),
        out_specs=(P(("gx", "gy")), P(("gx", "gy"), None), P(("gx", "gy"), None)),
        check_vma=False,
    )
```

```python
import functools

import jax
import jax.numpy as jnp
from jax import lax
from jax.experimental import pallas as pl
from jax.experimental.pallas import tpu as pltpu
from jax.sharding import PartitionSpec as P

STEPS = 4
MESH = pl.DeviceIdType.MESH
F32 = jnp.float32
BF16 = jnp.bfloat16
CHUNKS = 2
TAIL = 4
NT = ((1,), (1,))
NN = ((1,), (0,))


def split(x):
    high = x.astype(BF16)
    return high, (x - high.astype(F32)).astype(BF16)


def dot(a, b, dims):
    return lax.dot_general(a, b, (dims, ((), ())), preferred_element_type=F32)


def dot3(a, b, dims):
    return dot(a[0], b[0], dims) + (dot(a[0], b[1], dims) + dot(a[1], b[0], dims))


def kernel(
    nx, ny, images, texts, scalars, row_loss, image_grad, text_grad,
    held, high, low, grad, loss, load_sem, send_sem, recv_sem,
):
    rows, width = images.shape
    part = rows // CHUNKS
    total = nx * ny
    me = lax.axis_index("gx") * ny + lax.axis_index("gy")
    core = lax.rem(me, 2)
    sign = 1 - 2 * core

    def at(p):
        p = lax.rem(p + total, total)
        return (p // ny, lax.rem(p, ny))

    mate, behind = at(me + sign), at(me - sign)
    ahead, back2 = at(me + 2 * sign), at(me - 2 * sign)

    loads = [
        pltpu.make_async_copy(texts, held.at[0, 0], load_sem.at[0]),
        pltpu.make_async_copy(images, held.at[1, 0], load_sem.at[1]),
    ]
    for load in loads:
        load.start()

    barrier = pltpu.get_barrier_semaphore()
    for device in (mate, behind, back2):
        pl.semaphore_signal(barrier, inc=1, device_id=device, device_id_type=MESH)
    pl.semaphore_wait(barrier, 3)

    def copy(kind, stream, source, target, chunk, device, size=part):
        here = pl.ds(chunk * size, size)
        if source is None:
            source = held.at[stream, target - 1]
        return pltpu.make_async_remote_copy(
            src_ref=source.at[here],
            dst_ref=held.at[stream, target, here],
            send_sem=send_sem.at[kind, chunk],
            recv_sem=recv_sem.at[stream, target, chunk],
            device_id=device,
            device_id_type=MESH,
        )

    def own_to_next(chunk, mine, other):
        return copy(0, 1 - core, other, 1, chunk, behind)

    def own_to_ahead(chunk, mine, other):
        return copy(1, core, mine, 2, chunk, ahead)

    def own_to_mate(chunk, mine, other):
        return copy(2, core, mine, 1, chunk, mate)

    def pass_ahead(chunk):
        return copy(3, core, held.at[core, 1], 3, chunk, ahead, rows // TAIL)

    def relay_first(chunk):
        return copy(4, core, held.at[core, 1], 2, chunk, mate)

    def relay_second(chunk):
        return copy(5, core, held.at[core, 2], 3, chunk, mate)

    for which, mine, other in ((0, texts, images), (1, images, texts)):

        @pl.when(core == which)
        def _():
            for make in (own_to_next, own_to_ahead, own_to_mate):
                for chunk in range(CHUNKS):
                    make(chunk, mine, other).start()

    for load in loads:
        load.wait()
    for stream in range(2):
        high[stream], low[stream] = split(held[1 - stream, 0])
    grad[...] = jnp.zeros_like(grad)
    loss[...] = jnp.zeros_like(loss)
    temp = jnp.exp(scalars[0:1, :])
    shift = scalars[1:2, :]

    def arrived(stream, slot, chunk, size=part):
        here = held.at[stream, slot, pl.ds(chunk * size, size)]
        pltpu.make_async_copy(here, here, recv_sem.at[stream, slot, chunk]).wait()

    def coefficients(logits, positive):
        wide = logits.shape[1]
        logits = temp[:, :wide] * logits + shift[:, :wide]
        small = jnp.exp(-jnp.abs(logits))
        sigmoid = jnp.where(logits >= 0, 1.0, small) / (1.0 + small)
        if positive is None:
            return jnp.maximum(logits, 0.0) + jnp.log1p(small), temp[:, :wide] * sigmoid
        signed = jnp.where(positive, -logits, logits)
        losses = jnp.maximum(signed, 0.0) + jnp.log1p(small)
        return losses, temp * jnp.where(positive, sigmoid - 1.0, sigmoid)

    def whole(block, carry):
        slot = block // 2
        stream = lax.rem(core + 1 + block, 2)
        for chunk in range(CHUNKS):

            @pl.when(block >= 2)
            def _():
                arrived(stream, slot, chunk)

            @pl.when(block == 3)
            def _():
                for piece in range(TAIL // CHUNKS):
                    pass_ahead(chunk * (TAIL // CHUNKS) + piece).start()
                relay_first(chunk).start()

            @pl.when(block == 5)
            def _():
                relay_second(chunk).start()

        other = split(held[stream, slot])
        logits = dot3((high[stream], low[stream]), other, NT)
        pieces = []
        for chunk in range(CHUNKS):
            here = slice(chunk * part, (chunk + 1) * part)
            row = lax.broadcasted_iota(jnp.int32, (rows, part), 0)
            column = lax.broadcasted_iota(jnp.int32, (rows, part), 1) + chunk * part
            positive = jnp.logical_and(row == column, slot == 0)
            losses, coeff = coefficients(logits[:, here], positive)
            loss[stream] += losses
            pieces.append(coeff)
        grad[stream] += dot3(split(jnp.concatenate(pieces, axis=1)), other, NN)
        return carry

    def last(piece, carry):
        size = rows // TAIL
        arrived(core, STEPS - 1, piece, size)
        start = pl.multiple_of(piece * size, size)
        far, near = split(held[core, STEPS - 1, pl.ds(start, size), :])
        both = dot(high[core], jnp.concatenate([far, near], axis=0), NT)
        logits = both[:, :size] + both[:, size:] + dot(low[core], far, NT)
        losses, coeff = coefficients(logits, None)
        loss[core, :, :size] += losses
        top, rest = split(coeff)
        grad[core] += dot(
            jnp.concatenate([top, rest, top], axis=1),
            jnp.concatenate([far, far, near], axis=0),
            NN,
        )
        return carry

    lax.fori_loop(0, 2 * STEPS - 1, whole, 0)
    lax.fori_loop(0, TAIL, last, 0)

    image_grad[...] = grad[0]
    text_grad[...] = grad[1]
    row_loss[...] = jnp.sum(loss[0].T, axis=0) / (STEPS * rows)
    for chunk in range(CHUNKS):
        for make in (own_to_next, own_to_ahead, own_to_mate):
            make(chunk, texts, texts).wait_send()
        for make in (relay_first, relay_second):
            make(chunk).wait_send()
    for piece in range(TAIL):
        pass_ahead(piece).wait_send()


def finish(losses, first, second, row_loss, image_grad, text_grad, sem):
    copies = [
        pltpu.make_async_copy(first, image_grad, sem.at[0]),
        pltpu.make_async_copy(second, text_grad, sem.at[1]),
        pltpu.make_async_copy(losses, row_loss, sem.at[2]),
    ]
    for copy in copies:
        copy.start()
    for copy in copies:
        copy.wait()


def solution(mesh):
    nx, ny = mesh.shape["gx"], mesh.shape["gy"]

    def per_device(images, texts, log_temp, bias):
        rows, width = images.shape
        part = rows // CHUNKS
        vmem = pl.BlockSpec(memory_space=pltpu.VMEM)
        hbm = pl.BlockSpec(memory_space=pltpu.HBM)
        shapes = (
            jax.ShapeDtypeStruct((rows,), F32),
            jax.ShapeDtypeStruct((rows, width), F32),
            jax.ShapeDtypeStruct((rows, width), F32),
        )
        results = pl.pallas_call(
            functools.partial(kernel, nx, ny),
            out_shape=shapes,
            in_specs=[hbm, hbm, vmem],
            out_specs=(vmem, vmem, vmem),
            scratch_shapes=[
                pltpu.VMEM((2, STEPS, rows, width), F32),
                pltpu.VMEM((2, rows, width), BF16),
                pltpu.VMEM((2, rows, width), BF16),
                pltpu.VMEM((2, rows, width), F32),
                pltpu.VMEM((2, rows, part), F32),
                pltpu.SemaphoreType.DMA((2,)),
                pltpu.SemaphoreType.DMA((6, TAIL)),
                pltpu.SemaphoreType.DMA((2, STEPS, TAIL)),
            ],
            compiler_params=pltpu.CompilerParams(
                collective_id=0, has_side_effects=True, vmem_limit_bytes=51 << 20
            ),
        )(images, texts, jnp.stack([jnp.broadcast_to(log_temp, (part,)), jnp.broadcast_to(bias, (part,))]))
        return pl.pallas_call(
            finish,
            out_shape=shapes,
            in_specs=[vmem] * 3,
            out_specs=(hbm, hbm, hbm),
            scratch_shapes=[pltpu.SemaphoreType.DMA((3,))],
            compiler_params=pltpu.CompilerParams(vmem_limit_bytes=8 << 20),
        )(*results)

    return jax.shard_map(
        per_device,
        mesh=mesh,
        in_specs=(P(("gx", "gy"), None), P(("gx", "gy"), None), P(), P()),
        out_specs=(P(("gx", "gy")), P(("gx", "gy"), None), P(("gx", "gy"), None)),
        check_vma=False,
    )
```

```python
import functools

import jax
import jax.numpy as jnp
from jax import lax
from jax.experimental import pallas as pl
from jax.experimental.pallas import tpu as pltpu
from jax.sharding import PartitionSpec as P

STEPS = 4
MESH = pl.DeviceIdType.MESH
F32 = jnp.float32
BF16 = jnp.bfloat16
CHUNKS = 2
PIECES = 4
NT = ((1,), (1,))
NN = ((1,), (0,))


def split(x):
    high = x.astype(BF16)
    return high, (x - high.astype(F32)).astype(BF16)


def dot(a, b, dims):
    return lax.dot_general(a, b, (dims, ((), ())), preferred_element_type=F32)


def dot3(a, b, dims):
    return dot(a[0], b[0], dims) + (dot(a[0], b[1], dims) + dot(a[1], b[0], dims))


def kernel(
    nx, ny, images, texts, scalars, row_loss, image_grad, text_grad,
    held, high, low, grad, loss, load_sem, send_sem, recv_sem,
):
    rows, width = images.shape
    part = rows // CHUNKS
    total = nx * ny
    me = lax.axis_index("gx") * ny + lax.axis_index("gy")
    core = lax.rem(me, 2)
    sign = 1 - 2 * core

    def at(p):
        p = lax.rem(p + total, total)
        return (p // ny, lax.rem(p, ny))

    mate, behind = at(me + sign), at(me - sign)
    ahead, back2 = at(me + 2 * sign), at(me - 2 * sign)

    loads = [
        pltpu.make_async_copy(texts, held.at[0, 0], load_sem.at[0]),
        pltpu.make_async_copy(images, held.at[1, 0], load_sem.at[1]),
    ]
    for load in loads:
        load.start()

    barrier = pltpu.get_barrier_semaphore()
    for device in (mate, behind, back2):
        pl.semaphore_signal(barrier, inc=1, device_id=device, device_id_type=MESH)
    pl.semaphore_wait(barrier, 3)

    def copy(kind, stream, source, target, chunk, device):
        here = pl.ds(chunk * part, part)
        if source is None:
            source = held.at[stream, target - 1]
        return pltpu.make_async_remote_copy(
            src_ref=source.at[here],
            dst_ref=held.at[stream, target, here],
            send_sem=send_sem.at[kind, chunk],
            recv_sem=recv_sem.at[stream, target, chunk],
            device_id=device,
            device_id_type=MESH,
        )

    def own_to_next(chunk, mine, other):
        return copy(0, 1 - core, other, 1, chunk, behind)

    def own_to_ahead(chunk, mine, other):
        return copy(1, core, mine, 2, chunk, ahead)

    def own_to_mate(chunk, mine, other):
        return copy(2, core, mine, 1, chunk, mate)

    def pass_ahead(chunk):
        return copy(3, core, held.at[core, 1], 3, chunk, ahead)

    def relay_first(chunk):
        return copy(4, core, held.at[core, 1], 2, chunk, mate)

    def relay_second(chunk):
        return copy(5, core, held.at[core, 2], 3, chunk, mate)

    for which, mine, other in ((0, texts, images), (1, images, texts)):

        @pl.when(core == which)
        def _():
            for make in (own_to_next, own_to_ahead, own_to_mate):
                for chunk in range(CHUNKS):
                    make(chunk, mine, other).start()

    for load in loads:
        load.wait()
    for stream in range(2):
        high[stream], low[stream] = split(held[1 - stream, 0])
    grad[...] = jnp.zeros_like(grad)
    loss[...] = jnp.zeros_like(loss)
    temp = jnp.exp(scalars[0:1, :])
    shift = scalars[1:2, :]

    def arrived(stream, slot, chunk):
        here = held.at[stream, slot, pl.ds(chunk * part, part)]
        pltpu.make_async_copy(here, here, recv_sem.at[stream, slot, chunk]).wait()

    def coefficients(logits, positive):
        logits = temp * logits + shift
        small = jnp.exp(-jnp.abs(logits))
        sigmoid = jnp.where(logits >= 0, 1.0, small) / (1.0 + small)
        if positive is None:
            return jnp.maximum(logits, 0.0) + jnp.log1p(small), temp * sigmoid
        signed = jnp.where(positive, -logits, logits)
        losses = jnp.maximum(signed, 0.0) + jnp.log1p(small)
        return losses, temp * jnp.where(positive, sigmoid - 1.0, sigmoid)

    def whole(block, carry):
        slot = block // 2
        stream = lax.rem(core + 1 + block, 2)
        for chunk in range(CHUNKS):

            @pl.when(block >= 2)
            def _():
                arrived(stream, slot, chunk)

            @pl.when(block == 3)
            def _():
                pass_ahead(chunk).start()
                relay_first(chunk).start()

            @pl.when(block == 5)
            def _():
                relay_second(chunk).start()

        other = split(held[stream, slot])
        logits = dot3((high[stream], low[stream]), other, NT)
        pieces = []
        for chunk in range(CHUNKS):
            here = slice(chunk * part, (chunk + 1) * part)
            row = lax.broadcasted_iota(jnp.int32, (rows, part), 0)
            column = lax.broadcasted_iota(jnp.int32, (rows, part), 1) + chunk * part
            positive = jnp.logical_and(row == column, slot == 0)
            losses, coeff = coefficients(logits[:, here], positive)
            loss[stream] += losses
            pieces.append(coeff)
        grad[stream] += dot3(split(jnp.concatenate(pieces, axis=1)), other, NN)
        return carry

    def last(chunk, carry):
        arrived(core, STEPS - 1, chunk)
        start = pl.multiple_of(chunk * part, part)
        far, near = split(held[core, STEPS - 1, pl.ds(start, part), :])
        both = dot(high[core], jnp.concatenate([far, near], axis=0), NT)
        logits = both[:, :part] + both[:, part:] + dot(low[core], far, NT)
        losses, coeff = coefficients(logits, None)
        loss[core] += losses
        top, rest = split(coeff)
        grad[core] += dot(
            jnp.concatenate([top, rest], axis=1), jnp.concatenate([far, far], axis=0), NN
        ) + dot(top, near, NN)
        return carry

    def hand_over(which, stream, result):
        @pl.when(which == stream)
        def _():
            result[...] = grad[stream]

    lax.fori_loop(0, 2 * STEPS - 1, whole, 0)
    hand_over(1 - core, 0, image_grad)
    hand_over(1 - core, 1, text_grad)
    lax.fori_loop(0, CHUNKS, last, 0)
    hand_over(core, 0, image_grad)
    hand_over(core, 1, text_grad)

    row_loss[...] = jnp.sum(loss[0].T, axis=0) / (STEPS * rows)
    for chunk in range(CHUNKS):
        for make in (own_to_next, own_to_ahead, own_to_mate):
            make(chunk, texts, texts).wait_send()
        for make in (pass_ahead, relay_first, relay_second):
            make(chunk).wait_send()


def finish(losses, first, second, row_loss, image_grad, text_grad, sem):
    size = first.shape[0] // PIECES
    copies = [pltpu.make_async_copy(losses, row_loss, sem.at[0, PIECES])]
    for piece in range(PIECES):
        here = pl.ds(piece * size, size)
        copies += [
            pltpu.make_async_copy(first.at[here], image_grad.at[here], sem.at[0, piece]),
            pltpu.make_async_copy(second.at[here], text_grad.at[here], sem.at[1, piece]),
        ]
    for copy in copies:
        copy.start()
    for copy in copies:
        copy.wait()


def solution(mesh):
    nx, ny = mesh.shape["gx"], mesh.shape["gy"]

    def per_device(images, texts, log_temp, bias):
        rows, width = images.shape
        part = rows // CHUNKS
        vmem = pl.BlockSpec(memory_space=pltpu.VMEM)
        hbm = pl.BlockSpec(memory_space=pltpu.HBM)
        shapes = (
            jax.ShapeDtypeStruct((rows,), F32),
            jax.ShapeDtypeStruct((rows, width), F32),
            jax.ShapeDtypeStruct((rows, width), F32),
        )
        results = pl.pallas_call(
            functools.partial(kernel, nx, ny),
            out_shape=shapes,
            in_specs=[hbm, hbm, vmem],
            out_specs=(vmem, vmem, vmem),
            scratch_shapes=[
                pltpu.VMEM((2, STEPS, rows, width), F32),
                pltpu.VMEM((2, rows, width), BF16),
                pltpu.VMEM((2, rows, width), BF16),
                pltpu.VMEM((2, rows, width), F32),
                pltpu.VMEM((2, rows, part), F32),
                pltpu.SemaphoreType.DMA((2,)),
                pltpu.SemaphoreType.DMA((6, CHUNKS)),
                pltpu.SemaphoreType.DMA((2, STEPS, CHUNKS)),
            ],
            compiler_params=pltpu.CompilerParams(
                collective_id=0, has_side_effects=True, vmem_limit_bytes=51 << 20
            ),
        )(images, texts, jnp.stack([jnp.broadcast_to(log_temp, (part,)), jnp.broadcast_to(bias, (part,))]))
        return pl.pallas_call(
            finish,
            out_shape=shapes,
            in_specs=[vmem] * 3,
            out_specs=(hbm, hbm, hbm),
            scratch_shapes=[pltpu.SemaphoreType.DMA((2, PIECES + 1))],
            compiler_params=pltpu.CompilerParams(vmem_limit_bytes=8 << 20),
        )(*results)

    return jax.shard_map(
        per_device,
        mesh=mesh,
        in_specs=(P(("gx", "gy"), None), P(("gx", "gy"), None), P(), P()),
        out_specs=(P(("gx", "gy")), P(("gx", "gy"), None), P(("gx", "gy"), None)),
        check_vma=False,
    )
```

```python
import functools

import jax
import jax.numpy as jnp
from jax import lax
from jax.experimental import pallas as pl
from jax.experimental.pallas import tpu as pltpu
from jax.sharding import PartitionSpec as P

STEPS = 4
MESH = pl.DeviceIdType.MESH
F32 = jnp.float32
BF16 = jnp.bfloat16
CHUNKS = 2
PIECES = 4
NT = ((1,), (1,))
NN = ((1,), (0,))


def split(x):
    high = x.astype(BF16)
    return high, (x - high.astype(F32)).astype(BF16)


def dot(a, b, dims):
    return lax.dot_general(a, b, (dims, ((), ())), preferred_element_type=F32)


def dot3(a, b, dims):
    return dot(a[0], b[0], dims) + (dot(a[0], b[1], dims) + dot(a[1], b[0], dims))


def kernel(
    nx, ny, images, texts, scalars, row_loss, image_grad, text_grad,
    held, high, low, grad, loss, load_sem, send_sem, recv_sem,
):
    rows, width = images.shape
    part = rows // CHUNKS
    total = nx * ny
    me = lax.axis_index("gx") * ny + lax.axis_index("gy")
    core = lax.rem(me, 2)
    sign = 1 - 2 * core

    def at(p):
        p = lax.rem(p + total, total)
        return (p // ny, lax.rem(p, ny))

    mate, behind = at(me + sign), at(me - sign)
    ahead, back2 = at(me + 2 * sign), at(me - 2 * sign)

    loads = [
        pltpu.make_async_copy(texts, held.at[0, 0], load_sem.at[0]),
        pltpu.make_async_copy(images, held.at[1, 0], load_sem.at[1]),
    ]
    for load in loads:
        load.start()

    barrier = pltpu.get_barrier_semaphore()
    for device in (mate, behind, back2):
        pl.semaphore_signal(barrier, inc=1, device_id=device, device_id_type=MESH)
    pl.semaphore_wait(barrier, 3)

    def copy(kind, stream, source, target, chunk, device):
        here = pl.ds(chunk * part, part)
        if source is None:
            source = held.at[stream, target - 1]
        return pltpu.make_async_remote_copy(
            src_ref=source.at[here],
            dst_ref=held.at[stream, target, here],
            send_sem=send_sem.at[kind, chunk],
            recv_sem=recv_sem.at[stream, target, chunk],
            device_id=device,
            device_id_type=MESH,
        )

    def own_to_next(chunk, mine, other):
        return copy(0, 1 - core, other, 1, chunk, behind)

    def own_to_ahead(chunk, mine, other):
        return copy(1, core, mine, 2, chunk, ahead)

    def own_to_mate(chunk, mine, other):
        return copy(2, core, mine, 1, chunk, mate)

    def pass_ahead(chunk):
        return copy(3, core, held.at[core, 1], 3, chunk, ahead)

    def relay_first(chunk):
        return copy(4, core, held.at[core, 1], 2, chunk, mate)

    def relay_second(chunk):
        return copy(5, core, held.at[core, 2], 3, chunk, mate)

    for which, mine, other in ((0, texts, images), (1, images, texts)):

        @pl.when(core == which)
        def _():
            for make in (own_to_mate, own_to_next, own_to_ahead):
                for chunk in range(CHUNKS):
                    make(chunk, mine, other).start()

    for load in loads:
        load.wait()
    for stream in range(2):
        high[stream], low[stream] = split(held[1 - stream, 0])
    grad[...] = jnp.zeros_like(grad)
    loss[...] = jnp.zeros_like(loss)
    temp = jnp.exp(scalars[0:1, :])
    shift = scalars[1:2, :]

    def arrived(stream, slot, chunk):
        here = held.at[stream, slot, pl.ds(chunk * part, part)]
        pltpu.make_async_copy(here, here, recv_sem.at[stream, slot, chunk]).wait()

    def coefficients(logits, positive):
        logits = temp * logits + shift
        small = jnp.exp(-jnp.abs(logits))
        sigmoid = jnp.where(logits >= 0, 1.0, small) / (1.0 + small)
        if positive is None:
            return jnp.maximum(logits, 0.0) + jnp.log1p(small), temp * sigmoid
        signed = jnp.where(positive, -logits, logits)
        losses = jnp.maximum(signed, 0.0) + jnp.log1p(small)
        return losses, temp * jnp.where(positive, sigmoid - 1.0, sigmoid)

    def whole(block, carry):
        slot = block // 2
        stream = lax.rem(core + 1 + block, 2)
        for chunk in range(CHUNKS):

            @pl.when(block >= 2)
            def _():
                arrived(stream, slot, chunk)

            @pl.when(block == 3)
            def _():
                pass_ahead(chunk).start()
                relay_first(chunk).start()

            @pl.when(block == 5)
            def _():
                relay_second(chunk).start()

        other = split(held[stream, slot])
        logits = dot3((high[stream], low[stream]), other, NT)
        pieces = []
        for chunk in range(CHUNKS):
            here = slice(chunk * part, (chunk + 1) * part)
            row = lax.broadcasted_iota(jnp.int32, (rows, part), 0)
            column = lax.broadcasted_iota(jnp.int32, (rows, part), 1) + chunk * part
            positive = jnp.logical_and(row == column, slot == 0)
            losses, coeff = coefficients(logits[:, here], positive)
            loss[stream] += losses
            pieces.append(coeff)
        grad[stream] += dot3(split(jnp.concatenate(pieces, axis=1)), other, NN)
        return carry

    def last(chunk, carry):
        arrived(core, STEPS - 1, chunk)
        start = pl.multiple_of(chunk * part, part)
        far, near = split(held[core, STEPS - 1, pl.ds(start, part), :])
        both = dot(high[core], jnp.concatenate([far, near], axis=0), NT)
        logits = both[:, :part] + both[:, part:] + dot(low[core], far, NT)
        losses, coeff = coefficients(logits, None)
        loss[core] += losses
        top, rest = split(coeff)
        grad[core] += dot(
            jnp.concatenate([top, rest], axis=1), jnp.concatenate([far, far], axis=0), NN
        ) + dot(top, near, NN)
        return carry

    def hand_over(which, stream, result):
        @pl.when(which == stream)
        def _():
            result[...] = grad[stream]

    lax.fori_loop(0, 2 * STEPS - 1, whole, 0)
    hand_over(1 - core, 0, image_grad)
    hand_over(1 - core, 1, text_grad)
    lax.fori_loop(0, CHUNKS, last, 0)
    hand_over(core, 0, image_grad)
    hand_over(core, 1, text_grad)

    row_loss[...] = jnp.sum(loss[0].T, axis=0) / (STEPS * rows)
    for chunk in range(CHUNKS):
        for make in (own_to_next, own_to_ahead, own_to_mate):
            make(chunk, texts, texts).wait_send()
        for make in (pass_ahead, relay_first, relay_second):
            make(chunk).wait_send()


def finish(losses, first, second, row_loss, image_grad, text_grad, sem):
    size = first.shape[0] // PIECES
    copies = [pltpu.make_async_copy(losses, row_loss, sem.at[0, PIECES])]
    for piece in range(PIECES):
        here = pl.ds(piece * size, size)
        copies += [
            pltpu.make_async_copy(first.at[here], image_grad.at[here], sem.at[0, piece]),
            pltpu.make_async_copy(second.at[here], text_grad.at[here], sem.at[1, piece]),
        ]
    for copy in copies:
        copy.start()
    for copy in copies:
        copy.wait()


def solution(mesh):
    nx, ny = mesh.shape["gx"], mesh.shape["gy"]

    def per_device(images, texts, log_temp, bias):
        rows, width = images.shape
        part = rows // CHUNKS
        vmem = pl.BlockSpec(memory_space=pltpu.VMEM)
        hbm = pl.BlockSpec(memory_space=pltpu.HBM)
        shapes = (
            jax.ShapeDtypeStruct((rows,), F32),
            jax.ShapeDtypeStruct((rows, width), F32),
            jax.ShapeDtypeStruct((rows, width), F32),
        )
        results = pl.pallas_call(
            functools.partial(kernel, nx, ny),
            out_shape=shapes,
            in_specs=[hbm, hbm, vmem],
            out_specs=(vmem, vmem, vmem),
            scratch_shapes=[
                pltpu.VMEM((2, STEPS, rows, width), F32),
                pltpu.VMEM((2, rows, width), BF16),
                pltpu.VMEM((2, rows, width), BF16),
                pltpu.VMEM((2, rows, width), F32),
                pltpu.VMEM((2, rows, part), F32),
                pltpu.SemaphoreType.DMA((2,)),
                pltpu.SemaphoreType.DMA((6, CHUNKS)),
                pltpu.SemaphoreType.DMA((2, STEPS, CHUNKS)),
            ],
            compiler_params=pltpu.CompilerParams(
                collective_id=0, has_side_effects=True, vmem_limit_bytes=51 << 20
            ),
        )(images, texts, jnp.stack([jnp.broadcast_to(log_temp, (part,)), jnp.broadcast_to(bias, (part,))]))
        return pl.pallas_call(
            finish,
            out_shape=shapes,
            in_specs=[vmem] * 3,
            out_specs=(hbm, hbm, hbm),
            scratch_shapes=[pltpu.SemaphoreType.DMA((2, PIECES + 1))],
            compiler_params=pltpu.CompilerParams(vmem_limit_bytes=8 << 20),
        )(*results)

    return jax.shard_map(
        per_device,
        mesh=mesh,
        in_specs=(P(("gx", "gy"), None), P(("gx", "gy"), None), P(), P()),
        out_specs=(P(("gx", "gy")), P(("gx", "gy"), None), P(("gx", "gy"), None)),
        check_vma=False,
    )
```
